128 devices in a mesh: worker: 16 (over x_lo, z, core), fsdp: 8 (over x_hi, y).
Axes of the slice: x: 4 (x_hi: 2, x_lo: 2; x = x_hi * 2 + x_lo), y: 4, z: 4, core: 2. Of those that a mesh axis runs over, the one named last changes fastest.
Arguments:
- tokens_x: bfloat16 [16384, 4096], P(('worker', 'fsdp')), may hold values from -24 to 24
- attn_out: bfloat16 [16384, 2048], P(('worker', 'fsdp')), may hold values from -24 to 24
- query_cot: bfloat16 [16384, 2048], P(('worker', 'fsdp')), may hold values from -0.5 to 0.5
- out_cot: bfloat16 [16384, 4096], P(('worker', 'fsdp')), may hold values from -0.5 to 0.5
- message_ids: int32 [16384], P(('worker', 'fsdp')), may hold values from 0 to 1023
- q_offset: float32 [16, 4096, 2048], P('worker', 'fsdp'), may hold values from -12 to 12
- q_first: bfloat16 [16, 4096, 2048], P('worker', 'fsdp'), may hold values from -1.5 to 1.5
- q_second: bfloat16 [16, 4096, 2048], P('worker', 'fsdp'), may hold values from 0.0009994507 to 0.099609375
- o_offset: float32 [16, 2048, 4096], P('worker', 'fsdp'), may hold values from -12 to 12
- o_first: bfloat16 [16, 2048, 4096], P('worker', 'fsdp'), may hold values from -1.5 to 1.5
- o_second: bfloat16 [16, 2048, 4096], P('worker', 'fsdp'), may hold values from 0.0009994507 to 0.099609375
- q_momentum: float32 [4096, 2048], P(('fsdp', 'worker')), may hold values from -6 to 6
- o_momentum: float32 [2048, 4096], P(('fsdp', 'worker')), may hold values from -6 to 6
Outputs:
- q_first_new: bfloat16 [16, 4096, 2048], P('worker', 'fsdp')
- o_first_new: bfloat16 [16, 2048, 4096], P('worker', 'fsdp')
- q_direction: float32 [4096, 2048], P(('fsdp', 'worker'))
- o_direction: float32 [2048, 4096], P(('fsdp', 'worker'))
- q_momentum_new: float32 [4096, 2048], P(('fsdp', 'worker'))
- o_momentum_new: float32 [2048, 4096], P(('fsdp', 'worker'))
The draws below stay inside these ranges and needn't reach their ends.
All inputs are finite; a program needn't handle non-finite values.
Results may differ from the reference program's by a relative error of at most 0.019.
Values may be sent and summed in bfloat16 or wider, within the bound.
A program may use at most 192 MiB of HBM per device.

```python
import math
import jax
import jax.numpy as jnp
from jax import lax

D = 4096
VOCAB = 1024
CONTROL = 256
STEP = 500
TOK_DEV = 128
HQ = 2048
TOKENS = 16384
N_WORKER = 16
N_FSDP = 8


def place_ends(values, own_key, smallest, largest):
    extent = values.shape
    index_at = [jax.random.randint(jax.random.fold_in(own_key, axis), (), 0, extent[axis]) for axis in range(len(extent))]
    values = values.at[tuple(index_at)].set(smallest)
    longest = extent.index(max(extent))
    index_at[longest] = (index_at[longest] + 1) % extent[longest]
    return values.at[tuple(index_at)].set(largest)


def with_spikes(values, own_key, source, target, shards_of, factor):
    def block_of(axis_at):
        return (jnp.arange(values.shape[axis_at]) // (values.shape[axis_at] // shards_of)).reshape((-1,) + (1,) * (values.ndim - 1 - axis_at))

    first = jax.random.permutation(own_key, shards_of)[block_of(target)]
    second = (block_of(target) + shards_of // 2) % shards_of
    return jnp.where((block_of(source) == first) | (block_of(source) == second), factor * values, values)


def level_of(key, extent, cuts, least, largest):
    factor_of = 1.0
    for position, parts in cuts:
        steps = jax.random.uniform(jax.random.fold_in(jax.random.fold_in(key, 6), position), (parts,), jnp.float32, least / len(cuts), largest / len(cuts))
        factor_of = factor_of * jnp.repeat(jnp.exp(steps), extent[position] // parts).reshape((-1,) + (1,) * (len(extent) - 1 - position))
    return factor_of


def normal_values(own_key, dims, deviation, reach, cuts=(), kind=jnp.bfloat16):
    drawn = deviation * jax.random.normal(own_key, dims, jnp.float32)
    if cuts:
        drawn = drawn * level_of(own_key, dims, cuts, -0.22, 0.18)
    return jnp.clip(drawn, -reach, reach).astype(kind)


def noise_with(rng, dims, deviation, limit, split, heavy, dtype=jnp.bfloat16):
    entries = deviation * jax.random.normal(rng, dims, jnp.float32)
    if split:
        entries = entries * level_of(rng, dims, split, -0.22, 0.18)
    return jnp.clip(with_spikes(entries, jax.random.fold_in(rng, 3), *heavy), -limit, limit).astype(dtype)


def setup_inputs(seed: int = 0) -> dict:
    splits = jax.random.split(jax.random.key(seed), 14)
    return {
        "tokens_x": noise_with(splits[0], (TOKENS, D), 1.0, 24.0, ((0, 128),), (0, 1, 128, 5.5)),
        "attn_out": noise_with(splits[1], (TOKENS, HQ), 1.0, 24.0, ((0, 128),), (0, 1, 128, 5.5)),
        "query_cot": normal_values(splits[2], (TOKENS, HQ), 0.0625, 0.5, ((0, 128),)),
        "out_cot": normal_values(splits[3], (TOKENS, D), 0.0625, 0.5, ((0, 128),)),
        "message_ids": place_ends(jax.random.randint(splits[4], (TOKENS,), 0, VOCAB), jax.random.fold_in(splits[4], 1), 0, VOCAB - 1).astype(jnp.int32),
        "q_offset": normal_values(splits[5], (N_WORKER, D, HQ), 2.0, 12.0, ((0, 16), (1, 8)), jnp.float32),
        "q_first": normal_values(splits[6], (N_WORKER, D, HQ), 0.25, 1.5, ((0, 16), (1, 8))),
        "q_second": jnp.clip(jnp.exp(math.log(0.099609375) - 4.6018058 * jax.random.uniform(splits[7], (N_WORKER, D, HQ), jnp.float32) ** level_of(splits[7], (N_WORKER, D, HQ), ((0, 16), (1, 8)), -0.2, 0.2)), 0.0009994507, 0.099609375).astype(jnp.bfloat16),
        "o_offset": normal_values(splits[8], (N_WORKER, HQ, D), 2.0, 12.0, ((0, 16), (1, 8)), jnp.float32),
        "o_first": normal_values(splits[9], (N_WORKER, HQ, D), 0.25, 1.5, ((0, 16), (1, 8))),
        "o_second": jnp.clip(jnp.exp(math.log(0.099609375) - 4.6018058 * jax.random.uniform(splits[10], (N_WORKER, HQ, D), jnp.float32) ** level_of(splits[10], (N_WORKER, HQ, D), ((0, 16), (1, 8)), -0.2, 0.2)), 0.0009994507, 0.099609375).astype(jnp.bfloat16),
        "q_momentum": normal_values(splits[11], (D, HQ), 1.0, 6.0, ((0, 128),), jnp.float32),
        "o_momentum": normal_values(splits[12], (HQ, D), 1.0, 6.0, ((0, 128),), jnp.float32),
    }


first_decay = 0.9
second_decay = 0.999
adam_eps = 1e-08
outer_mu = 0.9

def shard_partial(left, right):
    part = jnp.dot(left.T, right, preferred_element_type=jnp.float32)
    return lax.optimization_barrier(part.astype(jnp.bfloat16)).astype(jnp.float32)

def adam_moved(grads, offset, first, second):
    first_new = first_decay * first.astype(jnp.float32) + (1.0 - first_decay) * grads
    second_new = second_decay * second.astype(jnp.float32) + (1.0 - second_decay) * grads * grads
    first_hat = first_new / (1.0 - first_decay ** STEP)
    second_hat = second_new / (1.0 - second_decay ** STEP)
    moved = offset + first_hat / (jnp.sqrt(second_hat) + adam_eps)
    return (first_new.astype(jnp.bfloat16), moved)

def to_blocks(array):
    return array.reshape(N_WORKER, N_FSDP, TOK_DEV, array.shape[1])

def reference(tokens_x, attn_out, query_cot, out_cot, message_ids, q_offset, q_first, q_second, o_offset, o_first, o_second, q_momentum, o_momentum):
    loss_mask = (message_ids >= CONTROL).astype(jnp.bfloat16)[:, None]
    q_cot = query_cot * loss_mask
    o_cot = out_cot * loss_mask

    def worker_step(sums, inputs):
        x_rows, a_rows, qc_rows, oc_rows, off_q, mom_q, sec_q, off_o, mom_o, sec_o = inputs

        def device_step(grads, pieces):
            x_dev, a_dev, qc_dev, oc_dev = pieces
            return ((grads[0] + shard_partial(x_dev, qc_dev), grads[1] + shard_partial(a_dev, oc_dev)), None)
        start_grads = (jnp.zeros((D, HQ), jnp.float32), jnp.zeros((HQ, D), jnp.float32))
        (grad_q, grad_o), unused = lax.scan(device_step, start_grads, (x_rows, a_rows, qc_rows, oc_rows))
        new_q, moved_q = adam_moved(grad_q, off_q, mom_q, sec_q)
        new_o, moved_o = adam_moved(grad_o, off_o, mom_o, sec_o)
        return ((sums[0] + moved_q, sums[1] + moved_o), (new_q, new_o))
    start_sums = (jnp.zeros((D, HQ), jnp.float32), jnp.zeros((HQ, D), jnp.float32))
    (sum_q, sum_o), (q_first_new, o_first_new) = lax.scan(worker_step, start_sums, (to_blocks(tokens_x), to_blocks(attn_out), to_blocks(q_cot), to_blocks(o_cot), q_offset, q_first, q_second, o_offset, o_first, o_second))
    pseudo_q = sum_q / N_WORKER
    pseudo_o = sum_o / N_WORKER
    q_momentum_new = outer_mu * q_momentum + pseudo_q
    o_momentum_new = outer_mu * o_momentum + pseudo_o
    q_direction = pseudo_q + outer_mu * q_momentum_new
    o_direction = pseudo_o + outer_mu * o_momentum_new
    return (q_first_new, o_first_new, q_direction, o_direction, q_momentum_new, o_momentum_new)
```

```python
import jax
import jax.numpy as jnp
from jax import lax
from jax.experimental import pallas as pl
from jax.experimental.pallas import tpu as pltpu
from jax.sharding import PartitionSpec as P

CONTROL = 256
STEP = 500
TOK = 128

first_decay = 0.9
second_decay = 0.999
adam_eps = 1e-08
outer_mu = 0.9
workers = 16
first_fix = 1.0 / (1.0 - first_decay**STEP)
second_fix = 1.0 / (1.0 - second_decay**STEP)

f32, bf16 = jnp.float32, jnp.bfloat16
MESH = pl.DeviceIdType.MESH

CHUNKS = tuple(
    (kind, number * width, width) for number in range(8) for kind, width in (("q", 256), ("o", 512))
)
AHEAD = 4
FORWARD = 2
LATER = (3, 4, 6, 8)
GATHER, HALF, CORE, ZED, XLO, OWN = 0, 3, 4, 5, 8, 9
N_SEM = 10


class Side:
    pass


def kernel(*refs):
    n_in, n_out = 13, 6
    ids_ref, x_hbm, a_hbm, cq_hbm, co_hbm = refs[:5]
    qoff_hbm, qfir_hbm, qsec_hbm, ooff_hbm, ofir_hbm, osec_hbm, qmom_hbm, omom_hbm = refs[5:n_in]
    scratch = refs[n_in + n_out :]
    x_in, a_in, x_t, a_t, lhs_send, lhs_recv, load_sem, send_sem, recv_sem = scratch[:9]
    names = ("lhs", "cot", "half_s", "half_r", "grad", "off", "sec", "core_r", "z_s", "z_r", "x_s", "x_r", "mine")
    q, o = Side(), Side()
    for place, name in enumerate(names):
        setattr(q, name, scratch[9 + place])
        setattr(o, name, scratch[9 + len(names) + place])
    q.cot_hbm, o.cot_hbm = cq_hbm, co_hbm
    q.fir, o.fir, q.way, o.way, q.mom, o.mom = refs[n_in : n_in + n_out]

    w, f = lax.axis_index("worker"), lax.axis_index("fsdp")
    core, z, xl = w % 2, (w // 2) % 4, w // 8
    y, xh = f % 4, f // 4

    def device(xl=xl, z=z, core=core, xh=xh, y=y):
        return (xl * 8 + z * 2 + core, xh * 4 + y)

    ring = [device(y=(y + k) % 4) for k in (1, 2, 3)]
    across = device(xh=1 - xh)
    beside = device(y=3 - y)
    corner = device(xh=1 - xh, y=3 - y)
    halver = device(y=y + 1 - 2 * (y % 2))
    twin = device(core=1 - core)
    zeds = [device(z=(z + k) % 4) for k in (1, 2, 3)]
    near = device(xl=1 - xl)

    q.own, q.other, q.partner = xh, 1 - xh, across
    o.own, o.other, o.partner = y % 2, 1 - y % 2, halver
    q.slot, o.slot = y, xh * 2 + y // 2

    loads = [
        pltpu.make_async_copy(a, b, load_sem.at[i])
        for i, (a, b) in enumerate(
            (
                (a_hbm, a_in),
                (x_hbm, x_in),
                (ooff_hbm, o.off),
                (ofir_hbm, o.fir),
                (osec_hbm, o.sec),
                (qoff_hbm, q.off),
                (qfir_hbm, q.fir),
                (qsec_hbm, q.sec),
                (omom_hbm, o.mom),
                (qmom_hbm, q.mom),
            )
        )
    ]
    for load in loads[:2]:
        load.start()

    barrier = pltpu.get_barrier_semaphore()
    met = (*ring, across, corner, twin, *zeds, near)
    for other in met:
        pl.semaphore_signal(barrier, inc=1, device_id=other, device_id_type=MESH)

    def own_block(side, number, c0, cw):
        return pltpu.make_async_copy(
            side.cot_hbm.at[:, pl.ds(c0, cw)],
            side.cot.at[pl.ds(pl.multiple_of(side.slot * TOK, TOK), TOK), pl.ds(c0, cw)],
            recv_sem.at[number, OWN],
        )

    own_copies = [own_block(q if kind == "q" else o, n, c0, cw) for n, (kind, c0, cw) in enumerate(CHUNKS)]
    for copy in own_copies:
        copy.start()
    for load in loads[2:]:
        load.start()

    mask = (ids_ref[...] >= CONTROL).astype(f32)
    loads[0].wait()

    @pl.loop(0, 8)
    def _(part):
        rows = a_in[:, pl.ds(pl.multiple_of(part * 256, 256), 256)].astype(f32)
        a_t[part // 4, part % 4] = (rows.T * mask).astype(bf16)

    loads[1].wait()

    @pl.loop(0, 8)
    def _(part):
        rows = x_in[:, pl.ds(pl.multiple_of(part * 512, 512), 512)].astype(f32)
        x_t[part // 4, part % 4] = (rows.T * mask).astype(bf16)

    def lanes(slot):
        return pl.ds(pl.multiple_of(slot * TOK, TOK), TOK)

    mine = [
        pltpu.make_async_copy(a_t.at[xh, pl.ds(2 * (y // 2), 2)], o.lhs.at[:, :, lanes(o.slot)], lhs_send.at[6]),
        pltpu.make_async_copy(x_t.at[:, y], q.lhs.at[:, :, lanes(q.slot)], lhs_send.at[7]),
    ]
    for copy in mine:
        copy.start()

    pl.semaphore_wait(barrier, len(met))

    sent = []

    def send(src, dst, s, r, to):
        copy = pltpu.make_async_remote_copy(
            src_ref=src, dst_ref=dst, send_sem=s, recv_sem=r, device_id=to, device_id_type=MESH
        )
        copy.start()
        sent.append(copy)
        return copy

    o_lhs, q_lhs = [], []

    def send_o_lhs():
        for i, (to, xt, yt) in enumerate(((across, 1 - xh, y), (beside, xh, 3 - y), (corner, 1 - xh, 3 - y))):
            o_lhs.append(
                send(
                    a_t.at[xt, pl.ds(2 * (yt // 2), 2)],
                    o.lhs.at[:, :, lanes(o.slot)],
                    lhs_send.at[i],
                    lhs_recv.at[i],
                    to,
                )
            )

    def send_q_lhs():
        for i, to in enumerate(ring):
            q_lhs.append(
                send(
                    x_t.at[:, (y + i + 1) % 4],
                    q.lhs.at[:, :, lanes(q.slot)],
                    lhs_send.at[3 + i],
                    lhs_recv.at[3 + i],
                    to,
                )
            )

    gathers = {}
    halves, cores, zs, xs = {}, {}, {}, {}

    def gather(n):
        kind, c0, cw = CHUNKS[n]
        side = q if kind == "q" else o
        cols = pl.ds(c0, cw)
        src = side.cot_hbm.at[:, cols]
        dst = side.cot.at[pl.ds(pl.multiple_of(side.slot * TOK, TOK), TOK), cols]
        targets = ring if kind == "q" else (across, beside)
        gathers[n] = [
            send(src, dst, send_sem.at[n, GATHER + i], recv_sem.at[n, GATHER + i], to) for i, to in enumerate(targets)
        ]

    def forward(n):
        kind, c0, cw = CHUNKS[n]
        if kind == "q":
            return
        gathers[n][0].wait_recv()
        slot = (1 - xh) * 2 + y // 2
        block = o.cot.at[pl.ds(pl.multiple_of(slot * TOK, TOK), TOK), pl.ds(c0, cw)]
        gathers[n].append(send(block, block, send_sem.at[n, GATHER + 2], recv_sem.at[n, GATHER + 2], beside))

    def product(side, which, c0, cw, store):
        @pl.loop(0, cw // 256)
        def _(part):
            there = pl.ds(pl.multiple_of(c0 + part * 256, 256), 256)
            here = pl.ds(pl.multiple_of(part * 256, 256), 256)
            store(there, here, jnp.dot(side.lhs[which], side.cot[:, there], preferred_element_type=f32))

    lhs_ready = set()

    def partial(n):
        kind, c0, cw = CHUNKS[n]
        side = q if kind == "q" else o
        if kind not in lhs_ready:
            lhs_ready.add(kind)
            mine[1 if kind == "q" else 0].wait()
            for copy in q_lhs if kind == "q" else o_lhs:
                copy.wait_recv()
        own_copies[n].wait()
        for copy in gathers[n][0 if kind == "q" else 1 :]:
            copy.wait_recv()

        def store(there, here, value):
            side.half_s[:, there] = value.astype(bf16)

        product(side, side.other, c0, cw, store)
        cols = pl.ds(c0, cw)
        halves[n] = send(
            side.half_s.at[:, cols], side.half_r.at[:, cols], send_sem.at[n, HALF], recv_sem.at[n, HALF], side.partner
        )

    state_ready = set()

    def adam(n):
        kind, c0, cw = CHUNKS[n]
        side = q if kind == "q" else o
        block = 32 if kind == "q" else 16

        def store(there, here, value):
            side.grad[:, here] = value

        product(side, side.own, c0, cw, store)
        if kind not in state_ready:
            state_ready.add(kind)
            for load in loads[5:8] if kind == "q" else loads[2:5]:
                load.wait()
        halves[n].wait_recv()

        @pl.loop(0, 16)
        def _(b):
            for r in range(0, block, 16):
                rows = pl.ds(pl.multiple_of(b * block + r, 16), 16)
                for c in range(0, cw, min(cw, 512)):
                    cols = pl.ds(c0 + c, min(cw, 512))
                    at = (b // 2, b % 2, pl.ds(r, 16), cols)
                    grad = side.grad[rows, pl.ds(c, min(cw, 512))] + side.half_r[rows, cols].astype(f32)
                    first = first_decay * side.fir[at].astype(f32) + (1.0 - first_decay) * grad
                    second = second_decay * side.sec[at].astype(f32) + (1.0 - second_decay) * grad * grad
                    side.fir[at] = first.astype(bf16)
                    moved = side.off[at] + (first * first_fix) / (jnp.sqrt(second * second_fix) + adam_eps)
                    side.off[at] = moved

        cols = pl.ds(c0, cw)
        cores[n] = send(
            side.off.at[:, 1 - core, :, cols],
            side.core_r.at[:, :, cols],
            send_sem.at[n, CORE],
            recv_sem.at[n, CORE],
            twin,
        )

    def along_z(n):
        kind, c0, cw = CHUNKS[n]
        side = q if kind == "q" else o
        block = 32 if kind == "q" else 16
        cores[n].wait_recv()

        @pl.loop(0, 8)
        def _(b):
            for c in range(0, cw, min(cw, 512)):
                cols = pl.ds(c0 + c, min(cw, 512))
                side.z_s[b % 4, b // 4, :, cols] = (side.off[b, core, :, cols] + side.core_r[b, :, cols]).astype(bf16)

        cols = pl.ds(c0, cw)
        zs[n] = [
            send(
                side.z_s.at[(z + i + 1) % 4, :, :, cols],
                side.z_r.at[i, :, :, cols],
                send_sem.at[n, ZED + i],
                recv_sem.at[n, ZED + i],
                to,
            )
            for i, to in enumerate(zeds)
        ]

    def along_x(n):
        kind, c0, cw = CHUNKS[n]
        side = q if kind == "q" else o
        for copy in zs[n]:
            copy.wait_recv()

        def total(part, cols):
            at = part * 4 + z
            value = side.off[at, core, :, cols] + side.core_r[at, :, cols]
            for i in range(3):
                value = value + side.z_r[i, part, :, cols].astype(f32)
            return value

        for c in range(0, cw, min(cw, 512)):
            cols = pl.ds(c0 + c, min(cw, 512))
            side.x_s[:, cols] = total(1 - xl, cols).astype(bf16)
        cols = pl.ds(c0, cw)
        xs[n] = send(side.x_s.at[:, cols], side.x_r.at[:, cols], send_sem.at[n, XLO], recv_sem.at[n, XLO], near)
        for c in range(0, cw, min(cw, 512)):
            cols = pl.ds(c0 + c, min(cw, 512))
            side.mine[:, cols] = total(xl, cols)

    mom_ready = set()

    def outer(n):
        kind, c0, cw = CHUNKS[n]
        side = q if kind == "q" else o
        if kind not in mom_ready:
            mom_ready.add(kind)
            loads[9 if kind == "q" else 8].wait()
        xs[n].wait_recv()
        for c in range(0, cw, min(cw, 512)):
            cols = pl.ds(c0 + c, min(cw, 512))
            pseudo = (side.mine[:, cols] + side.x_r[:, cols].astype(f32)) / workers
            momentum = outer_mu * side.mom[:, cols] + pseudo
            side.mom[:, cols] = momentum
            side.way[:, cols] = pseudo + outer_mu * momentum

    count = len(CHUNKS)
    gather(0)
    send_q_lhs()
    send_o_lhs()
    for n in range(1, min(AHEAD, count)):
        gather(n)
    for n in range(FORWARD):
        forward(n)
    for step in range(count + max(LATER)):
        if step + AHEAD < count:
            gather(step + AHEAD)
        if step < count:
            partial(step)
        if step + FORWARD < count:
            forward(step + FORWARD)
        for stage, later in zip((adam, along_z, along_x, outer), LATER):
            if 0 <= step - later < count:
                stage(step - later)

    for copy in sent:
        copy.wait_send()


def write_out(*refs):
    sems = refs[12]
    copies = [pltpu.make_async_copy(refs[i], refs[6 + i], sems.at[i]) for i in range(6)]
    for copy in copies:
        copy.start()
    for copy in copies:
        copy.wait()


def per_device(
    tokens_x,
    attn_out,
    query_cot,
    out_cot,
    message_ids,
    q_offset,
    q_first,
    q_second,
    o_offset,
    o_first,
    o_second,
    q_momentum,
    o_momentum,
):
    count = len(CHUNKS)
    any_spec = pl.BlockSpec(memory_space=pl.ANY)

    def side_scratch(rows, cols, chunk):
        block = rows // 16
        return [
            pltpu.VMEM((2, rows, 4 * TOK), bf16),
            pltpu.VMEM((4 * TOK, cols), bf16),
            pltpu.VMEM((rows, cols), bf16),
            pltpu.VMEM((rows, cols), bf16),
            pltpu.VMEM((rows, chunk), f32),
            pltpu.VMEM((8, 2, block, cols), f32),
            pltpu.VMEM((8, 2, block, cols), bf16),
            pltpu.VMEM((8, block, cols), f32),
            pltpu.VMEM((4, 2, block, cols), bf16),
            pltpu.VMEM((3, 2, block, cols), bf16),
            pltpu.VMEM((block, cols), bf16),
            pltpu.VMEM((block, cols), bf16),
            pltpu.VMEM((block, cols), f32),
        ]

    outs = pl.pallas_call(
        kernel,
        out_shape=(
            pltpu.VMEM((8, 2, 32, 2048), bf16),
            pltpu.VMEM((8, 2, 16, 4096), bf16),
            pltpu.VMEM((32, 2048), f32),
            pltpu.VMEM((16, 4096), f32),
            pltpu.VMEM((32, 2048), f32),
            pltpu.VMEM((16, 4096), f32),
        ),
        in_specs=[pl.BlockSpec(memory_space=pltpu.VMEM)] + [any_spec] * 12,
        out_specs=(pl.BlockSpec(memory_space=pltpu.VMEM),) * 6,
        scratch_shapes=[
            pltpu.VMEM((TOK, 4096), bf16),
            pltpu.VMEM((TOK, 2048), bf16),
            pltpu.VMEM((2, 4, 512, TOK), bf16),
            pltpu.VMEM((2, 4, 256, TOK), bf16),
            pltpu.SemaphoreType.DMA((8,)),
            pltpu.SemaphoreType.DMA((8,)),
            pltpu.SemaphoreType.DMA((10,)),
            pltpu.SemaphoreType.DMA((count, N_SEM)),
            pltpu.SemaphoreType.DMA((count, N_SEM)),
            *side_scratch(512, 2048, 512),
            *side_scratch(256, 4096, 1024),
        ],
        compiler_params=pltpu.CompilerParams(
            collective_id=0, has_side_effects=True, vmem_limit_bytes=50 * 2**20
        ),
        cost_estimate=pl.CostEstimate(flops=2**32, bytes_accessed=28 * 2**20, transcendentals=2**22),
        name="diloco",
    )(
        message_ids.reshape(1, TOK),
        tokens_x,
        attn_out,
        query_cot,
        out_cot,
        q_offset.reshape(8, 2, 32, 2048),
        q_first.reshape(8, 2, 32, 2048),
        q_second.reshape(8, 2, 32, 2048),
        o_offset.reshape(8, 2, 16, 4096),
        o_first.reshape(8, 2, 16, 4096),
        o_second.reshape(8, 2, 16, 4096),
        q_momentum,
        o_momentum,
    )
    outs = pl.pallas_call(
        write_out,
        out_shape=tuple(jax.ShapeDtypeStruct(out.shape, out.dtype) for out in outs),
        in_specs=[pl.BlockSpec(memory_space=pltpu.VMEM)] * 6,
        out_specs=(any_spec,) * 6,
        scratch_shapes=[pltpu.SemaphoreType.DMA((6,))],
        compiler_params=pltpu.CompilerParams(vmem_limit_bytes=2**20),
        name="write_out",
    )(*(pltpu.with_memory_space_constraint(out, pltpu.VMEM) for out in outs))
    return (outs[0].reshape(1, 512, 2048), outs[1].reshape(1, 256, 4096), *outs[2:])


def solution(mesh):
    tokens = P(("worker", "fsdp"), None)
    state = P("worker", "fsdp", None)
    share = P(("fsdp", "worker"), None)
    in_specs = (tokens,) * 4 + (P(("worker", "fsdp")),) + (state,) * 6 + (share,) * 2
    out_specs = (state,) * 2 + (share,) * 4
    return jax.shard_map(per_device, mesh=mesh, in_specs=in_specs, out_specs=out_specs, check_vma=False)
```

```python
import jax
import jax.numpy as jnp
from jax import lax
from jax.experimental import pallas as pl
from jax.experimental.pallas import tpu as pltpu
from jax.sharding import PartitionSpec as P

CONTROL = 256
STEP = 500
TOK = 128

first_decay = 0.9
second_decay = 0.999
adam_eps = 1e-08
outer_mu = 0.9
workers = 16
first_fix = 1.0 / (1.0 - first_decay**STEP)
second_fix = 1.0 / (1.0 - second_decay**STEP)

f32, bf16 = jnp.float32, jnp.bfloat16
MESH = pl.DeviceIdType.MESH

CHUNKS = tuple(
    (kind, number * width, width, how) for number in range(8) for kind, width, how in (("q", 256, "f"), ("o", 512, "y"))
)
CROSS_AHEAD = 12
AHEAD = 4
FORWARD = 2
LATER = (3, 4, 6, 8)
GATHER, HALF, CORE, ZED, XLO, OWN = 0, 4, 5, 6, 9, 10
N_SEM = 11


class Side:
    pass


def kernel(*refs):
    n_in, n_out = 13, 6
    ids_ref, x_hbm, a_hbm, cq_hbm, co_hbm = refs[:5]
    qoff_hbm, qfir_hbm, qsec_hbm, ooff_hbm, ofir_hbm, osec_hbm, qmom_hbm, omom_hbm = refs[5:n_in]
    scratch = refs[n_in + n_out :]
    x_in, a_in, x_t, a_t, lhs_send, lhs_recv, load_sem, send_sem, recv_sem = scratch[:9]
    names = ("lhs", "cot", "half_s", "half_r", "grad", "off", "sec", "core_r", "z_s", "z_r", "x_s", "x_r", "mine")
    q, o = Side(), Side()
    for place, name in enumerate(names):
        setattr(q, name, scratch[9 + place])
        setattr(o, name, scratch[9 + len(names) + place])
    q.cot_hbm, o.cot_hbm = cq_hbm, co_hbm
    q.fir, o.fir, q.way, o.way, q.mom, o.mom = refs[n_in : n_in + n_out]

    w, f = lax.axis_index("worker"), lax.axis_index("fsdp")
    core, z, xl = w % 2, (w // 2) % 4, w // 8
    y, xh = f % 4, f // 4

    def device(xl=xl, z=z, core=core, xh=xh, y=y):
        return (xl * 8 + z * 2 + core, xh * 4 + y)

    ring = [device(y=(y + k) % 4) for k in (1, 2, 3)]
    across = device(xh=1 - xh)
    beside = device(y=3 - y)
    corner = device(xh=1 - xh, y=3 - y)
    halver = device(y=y + 1 - 2 * (y % 2))
    twin = device(core=1 - core)
    zeds = [device(z=(z + k) % 4) for k in (1, 2, 3)]
    near = device(xl=1 - xl)

    q.own, q.other, q.partner = xh, 1 - xh, across
    o.own, o.other, o.partner = y % 2, 1 - y % 2, halver
    q.slot, o.slot = y, xh * 2 + y // 2

    loads = [
        pltpu.make_async_copy(a, b, load_sem.at[i])
        for i, (a, b) in enumerate(
            (
                (a_hbm, a_in),
                (x_hbm, x_in),
                (ooff_hbm, o.off),
                (ofir_hbm, o.fir),
                (osec_hbm, o.sec),
                (qoff_hbm, q.off),
                (qfir_hbm, q.fir),
                (qsec_hbm, q.sec),
                (omom_hbm, o.mom),
                (qmom_hbm, q.mom),
            )
        )
    ]
    for load in loads[:2]:
        load.start()

    barrier = pltpu.get_barrier_semaphore()
    met = (*ring, across, corner, twin, *zeds, near)
    for other in met:
        pl.semaphore_signal(barrier, inc=1, device_id=other, device_id_type=MESH)

    def own_block(side, number, c0, cw):
        return pltpu.make_async_copy(
            side.cot_hbm.at[:, pl.ds(c0, cw)],
            side.cot.at[pl.ds(pl.multiple_of(side.slot * TOK, TOK), TOK), pl.ds(c0, cw)],
            recv_sem.at[number, OWN],
        )

    own_copies = [own_block(q if kind == "q" else o, n, c0, cw) for n, (kind, c0, cw, _) in enumerate(CHUNKS)]
    for copy in own_copies:
        copy.start()
    for load in loads[2:]:
        load.start()

    mask = (ids_ref[...] >= CONTROL).astype(f32)
    loads[0].wait()

    @pl.loop(0, 8)
    def _(part):
        rows = a_in[:, pl.ds(pl.multiple_of(part * 256, 256), 256)].astype(f32)
        a_t[part // 4, part % 4] = (rows.T * mask).astype(bf16)

    loads[1].wait()

    @pl.loop(0, 8)
    def _(part):
        rows = x_in[:, pl.ds(pl.multiple_of(part * 512, 512), 512)].astype(f32)
        x_t[part // 4, part % 4] = (rows.T * mask).astype(bf16)

    def lanes(slot):
        return pl.ds(pl.multiple_of(slot * TOK, TOK), TOK)

    mine = [
        pltpu.make_async_copy(a_t.at[xh, pl.ds(2 * (y // 2), 2)], o.lhs.at[:, :, lanes(o.slot)], lhs_send.at[6]),
        pltpu.make_async_copy(x_t.at[:, y], q.lhs.at[:, :, lanes(q.slot)], lhs_send.at[7]),
    ]
    for copy in mine:
        copy.start()

    pl.semaphore_wait(barrier, len(met))

    sent = []

    def send(src, dst, s, r, to):
        copy = pltpu.make_async_remote_copy(
            src_ref=src, dst_ref=dst, send_sem=s, recv_sem=r, device_id=to, device_id_type=MESH
        )
        copy.start()
        sent.append(copy)
        return copy

    o_lhs, q_lhs = [], []

    def send_o_lhs():
        for i, (to, xt, yt) in enumerate(((across, 1 - xh, y), (beside, xh, 3 - y), (corner, 1 - xh, 3 - y))):
            o_lhs.append(
                send(
                    a_t.at[xt, pl.ds(2 * (yt // 2), 2)],
                    o.lhs.at[:, :, lanes(o.slot)],
                    lhs_send.at[i],
                    lhs_recv.at[i],
                    to,
                )
            )

    def send_q_lhs():
        for i, to in enumerate(ring):
            q_lhs.append(
                send(
                    x_t.at[:, (y + i + 1) % 4],
                    q.lhs.at[:, :, lanes(q.slot)],
                    lhs_send.at[3 + i],
                    lhs_recv.at[3 + i],
                    to,
                )
            )

    gathers = {}
    halves, cores, zs, xs = {}, {}, {}, {}

    def gather(n, i):
        kind, c0, cw, how = CHUNKS[n]
        side = q if kind == "q" else o
        cols = pl.ds(c0, cw)
        src = side.cot_hbm.at[:, cols]
        dst = side.cot.at[pl.ds(pl.multiple_of(side.slot * TOK, TOK), TOK), cols]
        to = {"d": ring, "f": (ring[0], ring[2])}.get(how, (across, beside))[i]
        gathers.setdefault(n, []).append(
            send(src, dst, send_sem.at[n, GATHER + i], recv_sem.at[n, GATHER + i], to)
        )

    def cross(n):
        if CHUNKS[n][0] == "o":
            gather(n, 0)

    def beside_or_ring(n):
        for i in {"d": (0, 1, 2), "f": (0, 1)}.get(CHUNKS[n][3], (1,)):
            gather(n, i)

    def forward(n):
        kind, c0, cw, how = CHUNKS[n]
        side = q if kind == "q" else o
        if how == "d":
            return
        if how == "f":
            passed = [((y + 3) % 4 * TOK, 64, ring[0]), ((y + 1) % 4 * TOK + 64, 64, ring[2])]
        elif how == "y":
            passed = [(((1 - xh) * 2 + y // 2) * TOK, TOK, beside)]
        else:
            passed = [((xh * 2 + 1 - y // 2) * TOK, TOK, across)]
        first = 1 if how == "x" else 0
        for i, (row, rows, to) in enumerate(passed):
            gathers[n][first + i].wait_recv()
            block = side.cot.at[pl.ds(pl.multiple_of(row, 64), rows), pl.ds(c0, cw)]
            at = GATHER + 2 + i
            gathers[n].append(send(block, block, send_sem.at[n, at], recv_sem.at[n, at], to))

    def product(side, which, c0, cw, store):
        wide = min(cw, 256)

        @pl.loop(0, cw // wide)
        def _(part):
            there = pl.ds(pl.multiple_of(c0 + part * wide, wide), wide)
            here = pl.ds(pl.multiple_of(part * wide, wide), wide)
            store(there, here, jnp.dot(side.lhs[which], side.cot[:, there], preferred_element_type=f32))

    lhs_ready = set()

    def partial(n):
        kind, c0, cw, how = CHUNKS[n]
        side = q if kind == "q" else o
        if kind not in lhs_ready:
            lhs_ready.add(kind)
            mine[1 if kind == "q" else 0].wait()
            for copy in q_lhs if kind == "q" else o_lhs:
                copy.wait_recv()
        own_copies[n].wait()
        for copy in {"d": gathers[n], "f": gathers[n][2:], "y": gathers[n][1:], "x": gathers[n][::2]}[how]:
            copy.wait_recv()

        def store(there, here, value):
            side.half_s[:, there] = value.astype(bf16)

        product(side, side.other, c0, cw, store)
        cols = pl.ds(c0, cw)
        halves[n] = send(
            side.half_s.at[:, cols], side.half_r.at[:, cols], send_sem.at[n, HALF], recv_sem.at[n, HALF], side.partner
        )

    state_ready = set()

    def adam(n):
        kind, c0, cw, how = CHUNKS[n]
        side = q if kind == "q" else o
        block = 32 if kind == "q" else 16

        def store(there, here, value):
            side.grad[:, here] = value

        product(side, side.own, c0, cw, store)
        if kind not in state_ready:
            state_ready.add(kind)
            for load in loads[5:8] if kind == "q" else loads[2:5]:
                load.wait()
        halves[n].wait_recv()

        @pl.loop(0, 16)
        def _(b):
            for r in range(0, block, 16):
                rows = pl.ds(pl.multiple_of(b * block + r, 16), 16)
                for c in range(0, cw, min(cw, 512)):
                    cols = pl.ds(c0 + c, min(cw, 512))
                    at = (b // 2, b % 2, pl.ds(r, 16), cols)
                    grad = side.grad[rows, pl.ds(c, min(cw, 512))] + side.half_r[rows, cols].astype(f32)
                    first = first_decay * side.fir[at].astype(f32) + (1.0 - first_decay) * grad
                    second = second_decay * side.sec[at].astype(f32) + (1.0 - second_decay) * grad * grad
                    side.fir[at] = first.astype(bf16)
                    moved = side.off[at] + (first * first_fix) / (jnp.sqrt(second * second_fix) + adam_eps)
                    side.off[at] = moved

        cols = pl.ds(c0, cw)
        cores[n] = send(
            side.off.at[:, 1 - core, :, cols],
            side.core_r.at[:, :, cols],
            send_sem.at[n, CORE],
            recv_sem.at[n, CORE],
            twin,
        )

    def along_z(n):
        kind, c0, cw, how = CHUNKS[n]
        side = q if kind == "q" else o
        block = 32 if kind == "q" else 16
        cores[n].wait_recv()

        @pl.loop(0, 8)
        def _(b):
            for c in range(0, cw, min(cw, 512)):
                cols = pl.ds(c0 + c, min(cw, 512))
                side.z_s[b % 4, b // 4, :, cols] = (side.off[b, core, :, cols] + side.core_r[b, :, cols]).astype(bf16)

        cols = pl.ds(c0, cw)
        zs[n] = [
            send(
                side.z_s.at[(z + i + 1) % 4, :, :, cols],
                side.z_r.at[i, :, :, cols],
                send_sem.at[n, ZED + i],
                recv_sem.at[n, ZED + i],
                to,
            )
            for i, to in enumerate(zeds)
        ]

    def along_x(n):
        kind, c0, cw, how = CHUNKS[n]
        side = q if kind == "q" else o
        for copy in zs[n]:
            copy.wait_recv()

        def total(part, cols):
            at = part * 4 + z
            value = side.off[at, core, :, cols] + side.core_r[at, :, cols]
            for i in range(3):
                value = value + side.z_r[i, part, :, cols].astype(f32)
            return value

        for c in range(0, cw, min(cw, 512)):
            cols = pl.ds(c0 + c, min(cw, 512))
            side.x_s[:, cols] = total(1 - xl, cols).astype(bf16)
        cols = pl.ds(c0, cw)
        xs[n] = send(side.x_s.at[:, cols], side.x_r.at[:, cols], send_sem.at[n, XLO], recv_sem.at[n, XLO], near)
        for c in range(0, cw, min(cw, 512)):
            cols = pl.ds(c0 + c, min(cw, 512))
            side.mine[:, cols] = total(xl, cols)

    mom_ready = set()

    def outer(n):
        kind, c0, cw, how = CHUNKS[n]
        side = q if kind == "q" else o
        if kind not in mom_ready:
            mom_ready.add(kind)
            loads[9 if kind == "q" else 8].wait()
        xs[n].wait_recv()
        for c in range(0, cw, min(cw, 512)):
            cols = pl.ds(c0 + c, min(cw, 512))
            pseudo = (side.mine[:, cols] + side.x_r[:, cols].astype(f32)) / workers
            momentum = outer_mu * side.mom[:, cols] + pseudo
            side.mom[:, cols] = momentum
            side.way[:, cols] = pseudo + outer_mu * momentum

    count = len(CHUNKS)
    cross(0)
    beside_or_ring(0)
    send_q_lhs()
    send_o_lhs()
    for n in range(1, min(CROSS_AHEAD, count)):
        cross(n)
        if n < AHEAD:
            beside_or_ring(n)
    for n in range(FORWARD):
        forward(n)
    for step in range(count + max(LATER)):
        if step + CROSS_AHEAD < count:
            cross(step + CROSS_AHEAD)
        if step + AHEAD < count:
            beside_or_ring(step + AHEAD)
        if step < count:
            partial(step)
        if step + FORWARD < count:
            forward(step + FORWARD)
        for stage, later in zip((adam, along_z, along_x, outer), LATER):
            if 0 <= step - later < count:
                stage(step - later)

    for copy in sent:
        copy.wait_send()


def write_out(*refs):
    sems = refs[12]
    copies = [pltpu.make_async_copy(refs[i], refs[6 + i], sems.at[i]) for i in range(6)]
    for copy in copies:
        copy.start()
    for copy in copies:
        copy.wait()


def per_device(
    tokens_x,
    attn_out,
    query_cot,
    out_cot,
    message_ids,
    q_offset,
    q_first,
    q_second,
    o_offset,
    o_first,
    o_second,
    q_momentum,
    o_momentum,
):
    count = len(CHUNKS)
    any_spec = pl.BlockSpec(memory_space=pl.ANY)

    def side_scratch(rows, cols, chunk):
        block = rows // 16
        return [
            pltpu.VMEM((2, rows, 4 * TOK), bf16),
            pltpu.VMEM((4 * TOK, cols), bf16),
            pltpu.VMEM((rows, cols), bf16),
            pltpu.VMEM((rows, cols), bf16),
            pltpu.VMEM((rows, chunk), f32),
            pltpu.VMEM((8, 2, block, cols), f32),
            pltpu.VMEM((8, 2, block, cols), bf16),
            pltpu.VMEM((8, block, cols), f32),
            pltpu.VMEM((4, 2, block, cols), bf16),
            pltpu.VMEM((3, 2, block, cols), bf16),
            pltpu.VMEM((block, cols), bf16),
            pltpu.VMEM((block, cols), bf16),
            pltpu.VMEM((block, cols), f32),
        ]

    outs = pl.pallas_call(
        kernel,
        out_shape=(
            pltpu.VMEM((8, 2, 32, 2048), bf16),
            pltpu.VMEM((8, 2, 16, 4096), bf16),
            pltpu.VMEM((32, 2048), f32),
            pltpu.VMEM((16, 4096), f32),
            pltpu.VMEM((32, 2048), f32),
            pltpu.VMEM((16, 4096), f32),
        ),
        in_specs=[pl.BlockSpec(memory_space=pltpu.VMEM)] + [any_spec] * 12,
        out_specs=(pl.BlockSpec(memory_space=pltpu.VMEM),) * 6,
        scratch_shapes=[
            pltpu.VMEM((TOK, 4096), bf16),
            pltpu.VMEM((TOK, 2048), bf16),
            pltpu.VMEM((2, 4, 512, TOK), bf16),
            pltpu.VMEM((2, 4, 256, TOK), bf16),
            pltpu.SemaphoreType.DMA((8,)),
            pltpu.SemaphoreType.DMA((8,)),
            pltpu.SemaphoreType.DMA((10,)),
            pltpu.SemaphoreType.DMA((count, N_SEM)),
            pltpu.SemaphoreType.DMA((count, N_SEM)),
            *side_scratch(512, 2048, 512),
            *side_scratch(256, 4096, 1024),
        ],
        compiler_params=pltpu.CompilerParams(
            collective_id=0, has_side_effects=True, vmem_limit_bytes=50 * 2**20
        ),
        cost_estimate=pl.CostEstimate(flops=2**32, bytes_accessed=28 * 2**20, transcendentals=2**22),
        name="diloco",
    )(
        message_ids.reshape(1, TOK),
        tokens_x,
        attn_out,
        query_cot,
        out_cot,
        q_offset.reshape(8, 2, 32, 2048),
        q_first.reshape(8, 2, 32, 2048),
        q_second.reshape(8, 2, 32, 2048),
        o_offset.reshape(8, 2, 16, 4096),
        o_first.reshape(8, 2, 16, 4096),
        o_second.reshape(8, 2, 16, 4096),
        q_momentum,
        o_momentum,
    )
    outs = pl.pallas_call(
        write_out,
        out_shape=tuple(jax.ShapeDtypeStruct(out.shape, out.dtype) for out in outs),
        in_specs=[pl.BlockSpec(memory_space=pltpu.VMEM)] * 6,
        out_specs=(any_spec,) * 6,
        scratch_shapes=[pltpu.SemaphoreType.DMA((6,))],
        compiler_params=pltpu.CompilerParams(vmem_limit_bytes=2**20),
        name="write_out",
    )(*(pltpu.with_memory_space_constraint(out, pltpu.VMEM) for out in outs))
    return (outs[0].reshape(1, 512, 2048), outs[1].reshape(1, 256, 4096), *outs[2:])


def solution(mesh):
    tokens = P(("worker", "fsdp"), None)
    state = P("worker", "fsdp", None)
    share = P(("fsdp", "worker"), None)
    in_specs = (tokens,) * 4 + (P(("worker", "fsdp")),) + (state,) * 6 + (share,) * 2
    out_specs = (state,) * 2 + (share,) * 4
    return jax.shard_map(per_device, mesh=mesh, in_specs=in_specs, out_specs=out_specs, check_vma=False)
```

```python
import jax
import jax.numpy as jnp
from jax import lax
from jax.experimental import pallas as pl
from jax.experimental.pallas import tpu as pltpu
from jax.sharding import PartitionSpec as P

CONTROL = 256
STEP = 500
TOK = 128

first_decay = 0.9
second_decay = 0.999
adam_eps = 1e-08
outer_mu = 0.9
workers = 16
first_fix = 1.0 / (1.0 - first_decay**STEP)
second_fix = 1.0 / (1.0 - second_decay**STEP)

f32, bf16 = jnp.float32, jnp.bfloat16
MESH = pl.DeviceIdType.MESH

CHUNKS = tuple(
    (kind, number * width, width, how) for number in range(8) for kind, width, how in (("q", 256, "f"), ("o", 512, "y"))
)
CROSS_AHEAD = 12
AHEAD = 3
FORWARD = 2
LATER = (3, 4, 6, 8)
GATHER, HALF, CORE, ZED, XLO, OWN = 0, 4, 5, 6, 9, 10
N_SEM = 11


class Side:
    pass


def kernel(*refs):
    n_in, n_out = 13, 6
    ids_ref, x_hbm, a_hbm, cq_hbm, co_hbm = refs[:5]
    qoff_hbm, qfir_hbm, qsec_hbm, ooff_hbm, ofir_hbm, osec_hbm, qmom_hbm, omom_hbm = refs[5:n_in]
    scratch = refs[n_in + n_out :]
    x_in, a_in, x_t, a_t, lhs_send, lhs_recv, load_sem, send_sem, recv_sem = scratch[:9]
    names = ("lhs", "cot", "half_s", "half_r", "grad", "off", "sec", "core_r", "z_s", "z_r", "x_s", "x_r", "mine")
    q, o = Side(), Side()
    for place, name in enumerate(names):
        setattr(q, name, scratch[9 + place])
        setattr(o, name, scratch[9 + len(names) + place])
    q.cot_hbm, o.cot_hbm = cq_hbm, co_hbm
    q.fir, o.fir, q.way, o.way, q.mom, o.mom = refs[n_in : n_in + n_out]

    w, f = lax.axis_index("worker"), lax.axis_index("fsdp")
    core, z, xl = w % 2, (w // 2) % 4, w // 8
    y, xh = f % 4, f // 4

    def device(xl=xl, z=z, core=core, xh=xh, y=y):
        return (xl * 8 + z * 2 + core, xh * 4 + y)

    ring = [device(y=(y + k) % 4) for k in (1, 2, 3)]
    across = device(xh=1 - xh)
    beside = device(y=3 - y)
    corner = device(xh=1 - xh, y=3 - y)
    halver = device(y=y + 1 - 2 * (y % 2))
    twin = device(core=1 - core)
    zeds = [device(z=(z + k) % 4) for k in (1, 2, 3)]
    near = device(xl=1 - xl)

    q.own, q.other, q.partner = xh, 1 - xh, across
    o.own, o.other, o.partner = y % 2, 1 - y % 2, halver
    q.slot, o.slot = y, xh * 2 + y // 2

    loads = [
        pltpu.make_async_copy(a, b, load_sem.at[i])
        for i, (a, b) in enumerate(
            (
                (a_hbm, a_in),
                (x_hbm, x_in),
                (ooff_hbm, o.off),
                (ofir_hbm, o.fir),
                (osec_hbm, o.sec),
                (qoff_hbm, q.off),
                (qfir_hbm, q.fir),
                (qsec_hbm, q.sec),
                (omom_hbm, o.mom),
                (qmom_hbm, q.mom),
            )
        )
    ]
    loads[1].start()
    loads[0].start()

    barrier = pltpu.get_barrier_semaphore()
    met = (*ring, across, corner, twin, *zeds, near)
    for other in met:
        pl.semaphore_signal(barrier, inc=1, device_id=other, device_id_type=MESH)

    def own_block(side, number, c0, cw):
        return pltpu.make_async_copy(
            side.cot_hbm.at[:, pl.ds(c0, cw)],
            side.cot.at[pl.ds(pl.multiple_of(side.slot * TOK, TOK), TOK), pl.ds(c0, cw)],
            recv_sem.at[number, OWN],
        )

    own_copies = [own_block(q if kind == "q" else o, n, c0, cw) for n, (kind, c0, cw, _) in enumerate(CHUNKS)]
    for copy in own_copies:
        copy.start()
    for load in loads[2:]:
        load.start()

    mask = (ids_ref[...] >= CONTROL).astype(f32)

    def turn(source, target, width, xt, yt):
        rows = source[:, pl.ds(pl.multiple_of((xt * 4 + yt) * width, width), width)].astype(f32)
        target[xt, yt] = (rows.T * mask).astype(bf16)

    loads[1].wait()

    @pl.loop(0, 6)
    def _(part):
        turn(x_in, x_t, 512, part % 2, (y + 1 + part // 2) % 4)

    pl.semaphore_wait(barrier, len(met))

    def lanes(slot):
        return pl.ds(pl.multiple_of(slot * TOK, TOK), TOK)

    mine = [
        pltpu.make_async_copy(a_t.at[xh, pl.ds(2 * (y // 2), 2)], o.lhs.at[:, :, lanes(o.slot)], lhs_send.at[6]),
        pltpu.make_async_copy(x_t.at[:, y], q.lhs.at[:, :, lanes(q.slot)], lhs_send.at[7]),
    ]
    sent = []

    def send(src, dst, s, r, to):
        copy = pltpu.make_async_remote_copy(
            src_ref=src, dst_ref=dst, send_sem=s, recv_sem=r, device_id=to, device_id_type=MESH
        )
        copy.start()
        sent.append(copy)
        return copy

    o_lhs, q_lhs = [], []

    def send_o_lhs():
        for i, (to, xt, yt) in enumerate(((across, 1 - xh, y), (beside, xh, 3 - y), (corner, 1 - xh, 3 - y))):
            o_lhs.append(
                send(
                    a_t.at[xt, pl.ds(2 * (yt // 2), 2)],
                    o.lhs.at[:, :, lanes(o.slot)],
                    lhs_send.at[i],
                    lhs_recv.at[i],
                    to,
                )
            )

    def send_q_lhs():
        for i, to in enumerate(ring):
            q_lhs.append(
                send(
                    x_t.at[:, (y + i + 1) % 4],
                    q.lhs.at[:, :, lanes(q.slot)],
                    lhs_send.at[3 + i],
                    lhs_recv.at[3 + i],
                    to,
                )
            )

    gathers = {}
    halves, cores, zs, xs = {}, {}, {}, {}

    def gather(n, i):
        kind, c0, cw, how = CHUNKS[n]
        side = q if kind == "q" else o
        cols = pl.ds(c0, cw)
        src = side.cot_hbm.at[:, cols]
        dst = side.cot.at[pl.ds(pl.multiple_of(side.slot * TOK, TOK), TOK), cols]
        to = {"d": ring, "f": (ring[0], ring[2])}.get(how, (across, beside))[i]
        gathers.setdefault(n, []).append(
            send(src, dst, send_sem.at[n, GATHER + i], recv_sem.at[n, GATHER + i], to)
        )

    def cross(n):
        if CHUNKS[n][0] == "o":
            gather(n, 0)

    def beside_or_ring(n):
        for i in {"d": (0, 1, 2), "f": (0, 1)}.get(CHUNKS[n][3], (1,)):
            gather(n, i)

    def forward(n):
        kind, c0, cw, how = CHUNKS[n]
        side = q if kind == "q" else o
        if how == "d":
            return
        if how == "f":
            passed = [((y + 3) % 4 * TOK, 64, ring[0]), ((y + 1) % 4 * TOK + 64, 64, ring[2])]
        elif how == "y":
            passed = [(((1 - xh) * 2 + y // 2) * TOK, TOK, beside)]
        else:
            passed = [((xh * 2 + 1 - y // 2) * TOK, TOK, across)]
        first = 1 if how == "x" else 0
        for i, (row, rows, to) in enumerate(passed):
            gathers[n][first + i].wait_recv()
            block = side.cot.at[pl.ds(pl.multiple_of(row, 64), rows), pl.ds(c0, cw)]
            at = GATHER + 2 + i
            gathers[n].append(send(block, block, send_sem.at[n, at], recv_sem.at[n, at], to))

    def product(side, which, c0, cw, store):
        wide = min(cw, 256)

        @pl.loop(0, cw // wide)
        def _(part):
            there = pl.ds(pl.multiple_of(c0 + part * wide, wide), wide)
            here = pl.ds(pl.multiple_of(part * wide, wide), wide)
            store(there, here, jnp.dot(side.lhs[which], side.cot[:, there], preferred_element_type=f32))

    lhs_ready = set()

    def partial(n):
        kind, c0, cw, how = CHUNKS[n]
        side = q if kind == "q" else o
        if kind not in lhs_ready:
            lhs_ready.add(kind)
            mine[1 if kind == "q" else 0].wait()
            for copy in q_lhs if kind == "q" else o_lhs:
                copy.wait_recv()
        own_copies[n].wait()
        for copy in {"d": gathers[n], "f": gathers[n][2:], "y": gathers[n][1:], "x": gathers[n][::2]}[how]:
            copy.wait_recv()

        def store(there, here, value):
            side.half_s[:, there] = value.astype(bf16)

        product(side, side.other, c0, cw, store)
        cols = pl.ds(c0, cw)
        halves[n] = send(
            side.half_s.at[:, cols], side.half_r.at[:, cols], send_sem.at[n, HALF], recv_sem.at[n, HALF], side.partner
        )

    state_ready = set()

    def adam(n):
        kind, c0, cw, how = CHUNKS[n]
        side = q if kind == "q" else o
        block = 32 if kind == "q" else 16

        def store(there, here, value):
            side.grad[:, here] = value

        product(side, side.own, c0, cw, store)
        if kind not in state_ready:
            state_ready.add(kind)
            for load in loads[5:8] if kind == "q" else loads[2:5]:
                load.wait()
        halves[n].wait_recv()

        @pl.loop(0, 16)
        def _(b):
            for r in range(0, block, 16):
                rows = pl.ds(pl.multiple_of(b * block + r, 16), 16)
                for c in range(0, cw, min(cw, 512)):
                    cols = pl.ds(c0 + c, min(cw, 512))
                    at = (b // 2, b % 2, pl.ds(r, 16), cols)
                    grad = side.grad[rows, pl.ds(c, min(cw, 512))] + side.half_r[rows, cols].astype(f32)
                    first = first_decay * side.fir[at].astype(f32) + (1.0 - first_decay) * grad
                    second = second_decay * side.sec[at].astype(f32) + (1.0 - second_decay) * grad * grad
                    side.fir[at] = first.astype(bf16)
                    moved = side.off[at] + (first * first_fix) / (jnp.sqrt(second * second_fix) + adam_eps)
                    side.off[at] = moved

        cols = pl.ds(c0, cw)
        cores[n] = send(
            side.off.at[:, 1 - core, :, cols],
            side.core_r.at[:, :, cols],
            send_sem.at[n, CORE],
            recv_sem.at[n, CORE],
            twin,
        )

    def along_z(n):
        kind, c0, cw, how = CHUNKS[n]
        side = q if kind == "q" else o
        block = 32 if kind == "q" else 16
        cores[n].wait_recv()

        @pl.loop(0, 8)
        def _(b):
            for c in range(0, cw, min(cw, 512)):
                cols = pl.ds(c0 + c, min(cw, 512))
                side.z_s[b % 4, b // 4, :, cols] = (side.off[b, core, :, cols] + side.core_r[b, :, cols]).astype(bf16)

        cols = pl.ds(c0, cw)
        zs[n] = [
            send(
                side.z_s.at[(z + i + 1) % 4, :, :, cols],
                side.z_r.at[i, :, :, cols],
                send_sem.at[n, ZED + i],
                recv_sem.at[n, ZED + i],
                to,
            )
            for i, to in enumerate(zeds)
        ]

    def along_x(n):
        kind, c0, cw, how = CHUNKS[n]
        side = q if kind == "q" else o
        for copy in zs[n]:
            copy.wait_recv()

        def total(part, cols):
            at = part * 4 + z
            value = side.off[at, core, :, cols] + side.core_r[at, :, cols]
            for i in range(3):
                value = value + side.z_r[i, part, :, cols].astype(f32)
            return value

        for c in range(0, cw, min(cw, 512)):
            cols = pl.ds(c0 + c, min(cw, 512))
            side.x_s[:, cols] = total(1 - xl, cols).astype(bf16)
        cols = pl.ds(c0, cw)
        xs[n] = send(side.x_s.at[:, cols], side.x_r.at[:, cols], send_sem.at[n, XLO], recv_sem.at[n, XLO], near)
        for c in range(0, cw, min(cw, 512)):
            cols = pl.ds(c0 + c, min(cw, 512))
            side.mine[:, cols] = total(xl, cols)

    mom_ready = set()

    def outer(n):
        kind, c0, cw, how = CHUNKS[n]
        side = q if kind == "q" else o
        if kind not in mom_ready:
            mom_ready.add(kind)
            loads[9 if kind == "q" else 8].wait()
        xs[n].wait_recv()
        for c in range(0, cw, min(cw, 512)):
            cols = pl.ds(c0 + c, min(cw, 512))
            pseudo = (side.mine[:, cols] + side.x_r[:, cols].astype(f32)) / workers
            momentum = outer_mu * side.mom[:, cols] + pseudo
            side.mom[:, cols] = momentum
            side.way[:, cols] = pseudo + outer_mu * momentum

    count = len(CHUNKS)
    cross(0)
    beside_or_ring(0)
    send_q_lhs()

    @pl.loop(0, 2)
    def _(part):
        turn(x_in, x_t, 512, part, y)

    mine[1].start()
    loads[0].wait()

    @pl.loop(0, 8)
    def _(part):
        turn(a_in, a_t, 256, part // 4, part % 4)

    mine[0].start()
    send_o_lhs()
    for n in range(1, min(CROSS_AHEAD, count)):
        cross(n)
        if n < AHEAD:
            beside_or_ring(n)
    for n in range(FORWARD):
        forward(n)
    for step in range(count + max(LATER)):
        if step + CROSS_AHEAD < count:
            cross(step + CROSS_AHEAD)
        if step + AHEAD < count:
            beside_or_ring(step + AHEAD)
        if step < count:
            partial(step)
        if step + FORWARD < count:
            forward(step + FORWARD)
        for stage, later in zip((adam, along_z, along_x, outer), LATER):
            if 0 <= step - later < count:
                stage(step - later)

    for copy in sent:
        copy.wait_send()


def write_out(*refs):
    sems = refs[12]
    copies = [pltpu.make_async_copy(refs[i], refs[6 + i], sems.at[i]) for i in range(6)]
    for copy in copies:
        copy.start()
    for copy in copies:
        copy.wait()


def per_device(
    tokens_x,
    attn_out,
    query_cot,
    out_cot,
    message_ids,
    q_offset,
    q_first,
    q_second,
    o_offset,
    o_first,
    o_second,
    q_momentum,
    o_momentum,
):
    count = len(CHUNKS)
    any_spec = pl.BlockSpec(memory_space=pl.ANY)

    def side_scratch(rows, cols, chunk):
        block = rows // 16
        return [
            pltpu.VMEM((2, rows, 4 * TOK), bf16),
            pltpu.VMEM((4 * TOK, cols), bf16),
            pltpu.VMEM((rows, cols), bf16),
            pltpu.VMEM((rows, cols), bf16),
            pltpu.VMEM((rows, chunk), f32),
            pltpu.VMEM((8, 2, block, cols), f32),
            pltpu.VMEM((8, 2, block, cols), bf16),
            pltpu.VMEM((8, block, cols), f32),
            pltpu.VMEM((4, 2, block, cols), bf16),
            pltpu.VMEM((3, 2, block, cols), bf16),
            pltpu.VMEM((block, cols), bf16),
            pltpu.VMEM((block, cols), bf16),
            pltpu.VMEM((block, cols), f32),
        ]

    outs = pl.pallas_call(
        kernel,
        out_shape=(
            pltpu.VMEM((8, 2, 32, 2048), bf16),
            pltpu.VMEM((8, 2, 16, 4096), bf16),
            pltpu.VMEM((32, 2048), f32),
            pltpu.VMEM((16, 4096), f32),
            pltpu.VMEM((32, 2048), f32),
            pltpu.VMEM((16, 4096), f32),
        ),
        in_specs=[pl.BlockSpec(memory_space=pltpu.VMEM)] + [any_spec] * 12,
        out_specs=(pl.BlockSpec(memory_space=pltpu.VMEM),) * 6,
        scratch_shapes=[
            pltpu.VMEM((TOK, 4096), bf16),
            pltpu.VMEM((TOK, 2048), bf16),
            pltpu.VMEM((2, 4, 512, TOK), bf16),
            pltpu.VMEM((2, 4, 256, TOK), bf16),
            pltpu.SemaphoreType.DMA((8,)),
            pltpu.SemaphoreType.DMA((8,)),
            pltpu.SemaphoreType.DMA((10,)),
            pltpu.SemaphoreType.DMA((count, N_SEM)),
            pltpu.SemaphoreType.DMA((count, N_SEM)),
            *side_scratch(512, 2048, 512),
            *side_scratch(256, 4096, 1024),
        ],
        compiler_params=pltpu.CompilerParams(
            collective_id=0, has_side_effects=True, vmem_limit_bytes=50 * 2**20
        ),
        cost_estimate=pl.CostEstimate(flops=2**32, bytes_accessed=28 * 2**20, transcendentals=2**22),
        name="diloco",
    )(
        message_ids.reshape(1, TOK),
        tokens_x,
        attn_out,
        query_cot,
        out_cot,
        q_offset.reshape(8, 2, 32, 2048),
        q_first.reshape(8, 2, 32, 2048),
        q_second.reshape(8, 2, 32, 2048),
        o_offset.reshape(8, 2, 16, 4096),
        o_first.reshape(8, 2, 16, 4096),
        o_second.reshape(8, 2, 16, 4096),
        q_momentum,
        o_momentum,
    )
    outs = pl.pallas_call(
        write_out,
        out_shape=tuple(jax.ShapeDtypeStruct(out.shape, out.dtype) for out in outs),
        in_specs=[pl.BlockSpec(memory_space=pltpu.VMEM)] * 6,
        out_specs=(any_spec,) * 6,
        scratch_shapes=[pltpu.SemaphoreType.DMA((6,))],
        compiler_params=pltpu.CompilerParams(vmem_limit_bytes=2**20),
        name="write_out",
    )(*(pltpu.with_memory_space_constraint(out, pltpu.VMEM) for out in outs))
    return (outs[0].reshape(1, 512, 2048), outs[1].reshape(1, 256, 4096), *outs[2:])


def solution(mesh):
    tokens = P(("worker", "fsdp"), None)
    state = P("worker", "fsdp", None)
    share = P(("fsdp", "worker"), None)
    in_specs = (tokens,) * 4 + (P(("worker", "fsdp")),) + (state,) * 6 + (share,) * 2
    out_specs = (state,) * 2 + (share,) * 4
    return jax.shard_map(per_device, mesh=mesh, in_specs=in_specs, out_specs=out_specs, check_vma=False)
```
